512 devices in a mesh: ctx: 64 (over y_hi, z, core), hs: 8 (over y_lo, x).
Axes of the slice: x: 4, y: 8 (y_hi: 4, y_lo: 2; y = y_hi * 2 + y_lo), z: 8, core: 2. Of those that a mesh axis runs over, the one named last changes fastest.
Arguments:
- queries: bfloat16 [8192, 36864], P('ctx', 'hs'), may hold values from -210 to 210
- grad_out: bfloat16 [8192, 32768], P('ctx', 'hs'), may hold values from -6 to 6
- prompt_kv: bfloat16 [576, 1024], P(None, 'hs'), may hold values from -6 to 6
- comp_kv: bfloat16 [576, 8192], P(None, 'ctx'), may hold values from -6 to 6
- lengths: int32 [64], replicated, may hold values from 32 to 128, as said below
Outputs:
- grad_queries: bfloat16 [8192, 36864], P('ctx', 'hs')
- grad_prompt: float32 [576, 1024], P(None, 'hs')
- grad_comp: float32 [576, 8192], P(None, 'ctx')
The draws below stay inside these ranges and needn't reach their ends.
Inputs may be any that keep to these rules, and one draw needn't show every extreme that they name: lengths[s] slots of completion s are live, the rest of its 128 slots are padding; some completion fills all 128 slots.
All inputs are finite; a program needn't handle non-finite values.
Results may differ from the reference program's by a relative error of at most 0.012.
Values may be sent and summed in bfloat16 or wider, within the bound.
No kernel may reach another device: no remote copies, remote signals or barrier semaphores. Data moves between devices by JAX's collectives and lax.ppermute only.
A program may use at most 64 MiB of HBM per device.

```python
import jax
import jax.numpy as jnp
from jax import lax

D_LAT = 512
D_ROPE = 64
HEADS = 64
CLEN = 128
DQK = 576
SAMPLES = 64
TOK = 8192
PROMPT = 1024


def shared_rotary(key):
    return jnp.clip(jax.random.normal(key, (D_ROPE, PROMPT), jnp.float32), -3.0, 3.0)


def draw_prompt_kv(key, part):
    rotary = shared_rotary(key)
    key = jax.random.fold_in(key, 11)
    latent = jnp.clip(jax.random.normal(key, (D_LAT, PROMPT), jnp.float32), -6.0, 6.0)
    return jnp.concatenate([latent, rotary], axis=0).astype(jnp.bfloat16)


def draw_queries(key, part):
    key = jax.random.fold_in(key, 12)
    base = jnp.clip(jax.random.normal(key, (TOK, HEADS, DQK), jnp.float32), -6.0, 6.0)
    return base.reshape(TOK, HEADS * DQK).astype(jnp.bfloat16)


def draw_lengths(key, part):
    key = jax.random.fold_in(key, 13)
    first_key, second_key = jax.random.split(key)
    drawn = jax.random.randint(first_key, (SAMPLES,), CLEN // 4, CLEN + 1, jnp.int32)
    chosen = jax.random.randint(second_key, (), 0, SAMPLES, jnp.int32)
    return drawn.at[chosen].set(CLEN)


def shard_levels(key, extent, cuts, least, high):
    def one(dim, shards_of):
        steps = jax.random.uniform(jax.random.fold_in(jax.random.fold_in(key, 6), dim), (shards_of,), jnp.float32, least / len(cuts), high / len(cuts))
        return jnp.repeat(jnp.exp(steps), extent[dim] // shards_of).reshape((-1,) + (1,) * (len(extent) - dim - 1))

    level = one(*cuts[0])
    for cut in cuts[1:]:
        level = level * one(*cut)
    return level


def scatter_about(rng, shape, deviation, bound, shards=(), kind=jnp.bfloat16):
    values = jax.random.normal(rng, shape, jnp.float32) * deviation
    if len(shards) > 0:
        values = shard_levels(rng, shape, shards, -0.22, 0.18) * values
    return jnp.clip(values, min=-bound, max=bound).astype(kind)


def setup_inputs(seed: int = 0) -> dict:
    seeds = jax.random.split(jax.random.key(seed), 6)
    queries = draw_queries(jax.random.fold_in(seeds[5], 71), 0)
    grad_out = scatter_about(seeds[1], (TOK, HEADS * D_LAT), 1.0, 6.0, ((0, 64), (1, 8)))
    prompt_kv = draw_prompt_kv(jax.random.fold_in(seeds[5], 71), 0)
    comp_kv = scatter_about(seeds[3], (DQK, TOK), 1.0, 6.0, ((1, 64),))
    lengths = draw_lengths(jax.random.fold_in(seeds[5], 71), 0)
    return {"queries": queries, "grad_out": grad_out, "prompt_kv": prompt_kv, "comp_kv": comp_kv, "lengths": lengths}


score_scale = 192.0 ** -0.5


def sample_grads(head_queries, cotangent, comp_keys, live_len, prompt_kv):
    keys_all = jnp.concatenate([prompt_kv, comp_keys], axis=1)
    values_all = keys_all[:D_LAT]
    keys_wide = keys_all.astype(jnp.float32)
    values_wide = values_all.astype(jnp.float32)
    queries_wide = head_queries.astype(jnp.float32)
    cotangent_wide = cotangent.astype(jnp.float32)
    position = jnp.arange(CLEN, dtype=jnp.int32)
    key_index = jnp.arange(PROMPT + CLEN, dtype=jnp.int32)
    allowed = key_index[None, :] < PROMPT + position[:, None] + 1
    scores = jnp.einsum("thd,dk->thk", queries_wide, keys_wide) * score_scale
    scores = jnp.where(allowed[:, None, :], scores, -jnp.inf)
    largest = jnp.max(scores, axis=-1, keepdims=True)
    weights = jnp.exp(scores - largest)
    probability = weights / jnp.sum(weights, axis=-1, keepdims=True)
    live_rows = (position < live_len).astype(jnp.float32)[:, None, None]
    live_prob = probability * live_rows
    kept_probs = live_prob.astype(jnp.bfloat16)
    kept_wide = kept_probs.astype(jnp.float32)
    grad_prob = jnp.einsum("the,ek->thk", cotangent_wide, values_wide)
    row_delta = jnp.sum(live_prob * grad_prob, axis=-1, keepdims=True)
    grad_score = (live_prob * (grad_prob - row_delta)).astype(jnp.bfloat16)
    score_wide = grad_score.astype(jnp.float32)
    grad_q = (jnp.einsum("thk,dk->thd", score_wide, keys_wide) * score_scale).astype(jnp.bfloat16)
    key_part = jnp.einsum("thk,thd->dk", score_wide, queries_wide) * score_scale
    value_part = jnp.einsum("thk,the->ek", kept_wide, cotangent_wide)
    key_grads = key_part + jnp.pad(value_part, ((0, D_ROPE), (0, 0)))
    return grad_q, key_grads[:, :PROMPT], key_grads[:, PROMPT:]


def reference(queries, grad_out, prompt_kv, comp_kv, lengths):
    query_blocks = queries.reshape(SAMPLES, CLEN, HEADS, DQK)
    grad_blocks = grad_out.reshape(SAMPLES, CLEN, HEADS, D_LAT)
    comp_blocks = comp_kv.reshape(DQK, SAMPLES, CLEN).transpose(1, 0, 2)

    def one_sample(running, inputs):
        grad_q, prompt_part, comp_part = sample_grads(inputs[0], inputs[1], inputs[2], inputs[3], prompt_kv)
        return running + prompt_part, (grad_q, comp_part)

    start = jnp.zeros((DQK, PROMPT), jnp.float32)
    total, stacked = lax.scan(one_sample, start, (query_blocks, grad_blocks, comp_blocks, lengths))
    grad_queries = stacked[0].reshape(TOK, HEADS * DQK)
    grad_comp = stacked[1].transpose(1, 0, 2).reshape(DQK, TOK)
    return grad_queries, total, grad_comp
```

```python
import jax
import jax.numpy as jnp
from jax import lax
from jax.sharding import Mesh
from jax.sharding import PartitionSpec as P

D_LAT = 512
DQK = 576
HS = ("yl", "x")
CTX = ("yh", "z", "c")


score_scale = 192.0 ** (-0.5)


def everyone(block, axes, count):
    copies = jnp.broadcast_to(block[None], (count,) + block.shape)
    return lax.all_to_all(copies, axes, 0, 0)


def on_device(queries, grad_out, prompt_kv, comp_kv, lengths):
    slot_count = queries.shape[0]
    head_count = queries.shape[1] // DQK
    head_queries = queries.reshape(slot_count, head_count, DQK)
    cotangent = grad_out.reshape(slot_count, head_count, D_LAT)
    sample = lax.axis_index(CTX)
    live_len = jnp.sum(jnp.where(jnp.arange(lengths.shape[0]) == sample, lengths, 0))
    gathered = everyone(prompt_kv, HS, 8)
    prompt_all = gathered.transpose(1, 0, 2).reshape(DQK, -1)
    prompt_len = prompt_all.shape[1]
    keys_all = jnp.concatenate([prompt_all, comp_kv], axis=1)
    values_all = keys_all[:D_LAT]
    position = jnp.arange(slot_count)
    key_index = jnp.arange(prompt_len + slot_count)
    allowed = key_index[None, :] < prompt_len + position[:, None] + 1
    scores = (
        jnp.einsum("thd,dk->thk", head_queries, keys_all, preferred_element_type=jnp.float32)
        * score_scale
    )
    scores = jnp.where(allowed[:, None, :], scores, -jnp.inf)
    largest = jnp.max(scores, axis=-1, keepdims=True)
    weights = jnp.exp(scores - largest)
    probability = weights / jnp.sum(weights, axis=-1, keepdims=True)
    live_rows = (position < live_len).astype(jnp.float32)[:, None, None]
    live_prob = probability * live_rows
    kept_probs = live_prob.astype(jnp.bfloat16)
    grad_prob = jnp.einsum("the,ek->thk", cotangent, values_all, preferred_element_type=jnp.float32)
    row_delta = jnp.sum(live_prob * grad_prob, axis=-1, keepdims=True)
    grad_score = (live_prob * (grad_prob - row_delta)).astype(jnp.bfloat16)
    grad_q = (
        jnp.einsum("thk,dk->thd", grad_score, keys_all, preferred_element_type=jnp.float32)
        * score_scale
    )
    grad_queries = grad_q.astype(jnp.bfloat16).reshape(slot_count, head_count * DQK)
    key_part = (
        jnp.einsum("thk,thd->dk", grad_score, head_queries, preferred_element_type=jnp.float32)
        * score_scale
    )
    value_part = jnp.einsum(
        "thk,the->ek", kept_probs, cotangent, preferred_element_type=jnp.float32
    )
    key_grads = key_part.at[:D_LAT].add(value_part)
    prompt_term = key_grads[:, :prompt_len].reshape(DQK, 8, -1).transpose(1, 0, 2)
    comp_term = key_grads[:, prompt_len:].reshape(8, DQK // 8, -1)
    terms = jnp.concatenate([prompt_term, comp_term], axis=1).astype(jnp.bfloat16)
    terms = lax.all_to_all(terms, HS, 0, 0)
    terms = jnp.sum(terms.astype(jnp.float32), axis=0).astype(jnp.bfloat16)
    comp_rows = everyone(terms[DQK:], HS, 8)
    grad_comp = comp_rows.reshape(DQK, -1).astype(jnp.float32)
    pieces = lax.all_to_all(terms[:DQK].reshape(8, DQK // 8, -1), "z", 0, 0)
    piece = jnp.sum(pieces.astype(jnp.float32), axis=0).astype(jnp.bfloat16)
    pieces = everyone(piece, ("yh", "c"), 8)
    piece = jnp.sum(pieces.astype(jnp.float32), axis=0).astype(jnp.bfloat16)
    grad_prompt = everyone(piece, "z", 8).reshape(DQK, -1).astype(jnp.float32)
    return (grad_queries, grad_prompt, grad_comp)


def solution(mesh):
    parts = Mesh(mesh.devices.reshape(4, 8, 2, 2, 4), CTX + HS)
    in_specs = (P(CTX, HS), P(CTX, HS), P(None, HS), P(None, CTX), P())
    out_specs = (P(CTX, HS), P(None, HS), P(None, CTX))
    return jax.shard_map(
        on_device, mesh=parts, in_specs=in_specs, out_specs=out_specs, check_vma=False
    )
```

```python
import functools

import jax
import jax.numpy as jnp
from jax import lax
from jax.experimental import pallas as pl
from jax.experimental.pallas import tpu as pltpu
from jax.sharding import Mesh
from jax.sharding import PartitionSpec as P

D_LAT = 512
DQK = 576
CLEN = 128
HEADS = 8
KEYS = 1152
PROMPT = 1024
ROWS = CLEN * HEADS
WIDE = 640
PIECE = 80
HS = ("yl", "x")
CTX = ("yh", "z", "c")
ORDER = (0, 2, 1, 3, 4, 6, 5, 7)

score_scale = 192.0 ** (-0.5)
LOG2E = 1.4426950408889634

BF = jnp.bfloat16
F32 = jnp.float32
VM = pl.BlockSpec(memory_space=pltpu.VMEM)
HBM = pl.BlockSpec(memory_space=pl.ANY)
PARAMS = pltpu.CompilerParams(vmem_limit_bytes=56 * 1024 * 1024)
SMALL = pltpu.CompilerParams(vmem_limit_bytes=4 * 1024 * 1024)


def dot(a, b, contract):
    return lax.dot_general(a, b, ((contract[0:1], contract[1:2]), ((), ())), preferred_element_type=F32)


def turn_kernel(q_ref, g_ref, left_ref):
    for i, h in enumerate(ORDER):
        part = q_ref[:, 1152 * (h // 2) + 512 * (h % 2) : 1152 * (h // 2) + 512 * (h % 2) + WIDE]
        turned = part.T
        first = 64 * (h % 2)
        left_ref[:, i * CLEN : (i + 1) * CLEN] = turned[first : first + DQK]
        left_ref[0:D_LAT, ROWS + i * CLEN : ROWS + (i + 1) * CLEN] = g_ref[:, D_LAT * h : D_LAT * (h + 1)].T
    left_ref[D_LAT:DQK, ROWS:] = jnp.zeros((DQK - D_LAT, ROWS), BF)


def turn(queries, grad_out):
    return pl.pallas_call(
        turn_kernel,
        out_shape=jax.ShapeDtypeStruct((DQK, 2 * ROWS), BF),
        in_specs=[VM, VM],
        out_specs=VM,
        compiler_params=PARAMS,
        cost_estimate=pl.CostEstimate(flops=0, bytes_accessed=4600000, transcendentals=0),
    )(queries, grad_out)


def fill_keys(prompt_ref, comp_ref, keys_ref, shift):
    zero = jnp.zeros((WIDE - DQK, KEYS), BF)
    if shift:
        keys_ref[0 : WIDE - DQK] = zero
    else:
        keys_ref[DQK:WIDE] = zero
    for j in range(8):
        keys_ref[shift : shift + DQK, j * CLEN : (j + 1) * CLEN] = prompt_ref[j]
    keys_ref[shift : shift + DQK, PROMPT:KEYS] = comp_ref[...]


def main_kernel(live_ref, q_hbm, g_hbm, left_hbm, prompt_hbm, comp_hbm, terms_hbm, score_grad_hbm, q_ref, g_ref, left_ref, right_ref, terms_ref, even_ref, odd_ref, score_ref, gprob_ref, in_sems, out_sems):
    zero = jnp.zeros((WIDE - DQK, KEYS), BF)
    even_ref[DQK:WIDE] = zero
    odd_ref[0 : WIDE - DQK] = zero

    def keys_in(ref, shift, sem):
        rows = pl.ds(shift, DQK)
        moves = [pltpu.make_async_copy(prompt_hbm.at[j], ref.at[rows, pl.ds(j * CLEN, CLEN)], sem) for j in range(8)]
        return moves + [pltpu.make_async_copy(comp_hbm, ref.at[rows, pl.ds(PROMPT, CLEN)], sem)]

    half_q, half_g = pl.ds(0, 2304), pl.ds(0, 2048)
    rest_q, rest_g = pl.ds(2304, 2304), pl.ds(2048, 2048)
    loads = [
        keys_in(even_ref, 0, in_sems.at[0]),
        [pltpu.make_async_copy(q_hbm.at[:, half_q], q_ref.at[:, half_q], in_sems.at[1])],
        [pltpu.make_async_copy(g_hbm.at[:, half_g], g_ref.at[:, half_g], in_sems.at[2])],
        keys_in(odd_ref, WIDE - DQK, in_sems.at[3]),
        [pltpu.make_async_copy(q_hbm.at[:, rest_q], q_ref.at[:, rest_q], in_sems.at[4])],
        [pltpu.make_async_copy(g_hbm.at[:, rest_g], g_ref.at[:, rest_g], in_sems.at[5])],
        [pltpu.make_async_copy(left_hbm, left_ref, in_sems.at[6])],
    ]
    for load in loads:
        for move in load:
            move.start()

    def arrived(*which):
        for i in which:
            for move in loads[i]:
                move.wait()

    live = live_ref[0]
    pairs = [ORDER[2 * b : 2 * b + 2] for b in range(4)]

    def matmuls(b):
        odd = pairs[b][0] % 2
        starts = [1152 * (h // 2) + 512 * odd for h in pairs[b]]
        q = jnp.concatenate([q_ref[:, s : s + WIDE] for s in starts], axis=0)
        g = jnp.concatenate([g_ref[:, D_LAT * h : D_LAT * (h + 1)] for h in pairs[b]], axis=0)
        keys = odd_ref if odd else even_ref
        first = (WIDE - DQK) * odd
        score_ref[256 * b : 256 * (b + 1)] = dot(q, keys[...], (1, 0))
        gprob_ref[256 * b : 256 * (b + 1)] = dot(g, keys[first : first + D_LAT], (1, 0))

    def softmax(b):
        for r in range(256 * b, 256 * (b + 1), 16):
            slot = r % CLEN + lax.broadcasted_iota(jnp.int32, (16, CLEN), 0)
            own = lax.broadcasted_iota(jnp.int32, (16, CLEN), 1)
            score = score_ref[r : r + 16]
            tail = jnp.where(own <= slot, score[:, PROMPT:], -jnp.inf)
            score = jnp.concatenate([score[:, :PROMPT], tail], axis=1)
            largest = jnp.max(score, axis=1, keepdims=True)
            weight = jnp.exp2((score - largest) * (score_scale * LOG2E))
            total = jnp.sum(weight, axis=1, keepdims=True)
            alive = (slot[:, :1] < live).astype(F32)
            prob = weight * (alive / total)
            gprob = gprob_ref[r : r + 16]
            delta = jnp.sum(prob * gprob, axis=1, keepdims=True)
            right_ref[r : r + 16] = (prob * ((gprob - delta) * score_scale)).astype(BF)
            right_ref[ROWS + r : ROWS + r + 16] = prob.astype(BF)

    outs = []

    def send(source, target, sem):
        outs.append(pltpu.make_async_copy(source, target, sem))
        outs[-1].start()

    arrived(0, 1, 2)
    matmuls(0)
    arrived(3)
    matmuls(1)
    softmax(0)
    arrived(4, 5)
    matmuls(2)
    softmax(1)
    matmuls(3)
    softmax(2)
    softmax(3)
    arrived(6)
    send(right_ref.at[pl.ds(0, ROWS)], score_grad_hbm, out_sems.at[4])
    for n, j in enumerate((PROMPT, 0, 256, 512, 768)):
        wide = min(256, KEYS - j)
        part = dot(left_ref[...], right_ref[:, j : j + wide], (1, 0)).astype(BF)
        if j < PROMPT:
            k = j // CLEN
            terms_ref[k, 0:DQK] = part[:, :CLEN]
            terms_ref[k + 1, 0:DQK] = part[:, CLEN:]
            send(terms_ref.at[pl.ds(k, 2)], terms_hbm.at[pl.ds(k, 2)], out_sems.at[n - 1])
        else:
            for k in range(8):
                rows = min(PIECE, DQK - PIECE * k)
                terms_ref[k, DQK : DQK + rows] = part[PIECE * k : PIECE * k + rows]
                if rows < PIECE:
                    terms_ref[k, DQK + rows : DQK + PIECE] = jnp.zeros((PIECE - rows, CLEN), BF)
    for move in outs:
        move.wait()


def main(live, queries, grad_out, left, prompt, comp):
    return pl.pallas_call(
        main_kernel,
        out_shape=(
            jax.ShapeDtypeStruct((8, DQK + PIECE, CLEN), BF),
            jax.ShapeDtypeStruct((ROWS, KEYS), BF),
        ),
        in_specs=[pl.BlockSpec(memory_space=pltpu.SMEM)] + [HBM] * 5,
        out_specs=(HBM, HBM),
        scratch_shapes=[
            pltpu.VMEM((CLEN, HEADS * DQK), BF),
            pltpu.VMEM((CLEN, HEADS * D_LAT), BF),
            pltpu.VMEM((DQK, 2 * ROWS), BF),
            pltpu.VMEM((2 * ROWS, KEYS), BF),
            pltpu.VMEM((8, DQK + PIECE, CLEN), BF),
            pltpu.VMEM((WIDE, KEYS), BF),
            pltpu.VMEM((WIDE, KEYS), BF),
            pltpu.VMEM((ROWS, KEYS), F32),
            pltpu.VMEM((ROWS, KEYS), F32),
            pltpu.SemaphoreType.DMA((7,)),
            pltpu.SemaphoreType.DMA((5,)),
        ],
        compiler_params=PARAMS,
        cost_estimate=pl.CostEstimate(flops=5200000000, bytes_accessed=12000000, transcendentals=1200000),
    )(live, queries, grad_out, left, prompt, comp)


def query_kernel(grad_ref, prompt_ref, comp_ref, out_ref, token_ref, even_ref, odd_ref):
    @pl.when(pl.program_id(0) == 0)
    def _():
        fill_keys(prompt_ref, comp_ref, even_ref, 0)
        fill_keys(prompt_ref, comp_ref, odd_ref, WIDE - DQK)
        token_ref[...] = jnp.zeros((16, CLEN), BF)

    even = dot(grad_ref[:256], even_ref[...], (1, 1))
    odd = dot(grad_ref[256:], odd_ref[...], (1, 1))
    for i in range(2):
        start = 1152 * i
        e, o = even[128 * i : 128 * (i + 1)], odd[128 * i : 128 * (i + 1)]
        out_ref[:, start : start + 512] = e[:, :512].astype(BF)
        out_ref[:, start + 512 : start + 640] = (e[:, 512:] + o[:, :128]).astype(BF)
        out_ref[:, start + 640 : start + 1152] = o[:, 128:].astype(BF)


def query_grads(score_grad, prompt, comp):
    return pl.pallas_call(
        query_kernel,
        out_shape=(jax.ShapeDtypeStruct((CLEN, HEADS * DQK), BF), jax.ShapeDtypeStruct((16, CLEN), BF)),
        grid=(2,),
        in_specs=[
            pl.BlockSpec((ROWS // 2, KEYS), lambda i: (i, 0)),
            pl.BlockSpec((8, DQK, CLEN), lambda i: (0, 0, 0)),
            pl.BlockSpec((DQK, CLEN), lambda i: (0, 0)),
        ],
        out_specs=(pl.BlockSpec((CLEN, HEADS * DQK // 2), lambda i: (0, i)), pl.BlockSpec((16, CLEN), lambda i: (0, 0))),
        scratch_shapes=[pltpu.VMEM((WIDE, KEYS), BF), pltpu.VMEM((WIDE, KEYS), BF)],
        compiler_params=PARAMS,
        cost_estimate=pl.CostEstimate(flops=1400000000, bytes_accessed=5000000, transcendentals=0),
    )(score_grad, prompt, comp)


def total_of(ref, first, rows):
    total = ref[0, first : first + rows].astype(F32)
    for j in range(1, ref.shape[0]):
        total = total + ref[j, first : first + rows].astype(F32)
    return total


def heads_sum_kernel(terms_ref, token_ref, prompt_ref, comp_ref):
    prompt_ref[0:DQK] = total_of(terms_ref, 0, DQK).astype(BF)
    prompt_ref[DQK:] = jnp.zeros((WIDE - DQK, CLEN), BF)
    comp_ref[...] = total_of(terms_ref, DQK, PIECE).astype(BF)


def heads_sum(terms, token):
    return pl.pallas_call(
        heads_sum_kernel,
        out_shape=(jax.ShapeDtypeStruct((WIDE, CLEN), BF), jax.ShapeDtypeStruct((PIECE, CLEN), BF)),
        in_specs=[VM, VM],
        out_specs=(VM, VM),
        compiler_params=SMALL,
        cost_estimate=pl.CostEstimate(flops=700000, bytes_accessed=1600000, transcendentals=0),
    )(terms, token)


def total_and_join_kernel(high_ref, pieces_ref, mine_ref, other_ref, out_ref, joined_ref):
    total = total_of(pieces_ref, 0, PIECE).astype(BF)
    for j in range(8):
        out_ref[j] = total
    join(high_ref[0], mine_ref, other_ref, joined_ref)


def join(high, mine_ref, other_ref, joined_ref):
    rows = mine_ref.shape[0]

    @pl.when(high == 0)
    def _():
        joined_ref[0:rows] = mine_ref[...].astype(joined_ref.dtype)
        joined_ref[rows:] = other_ref[...].astype(joined_ref.dtype)

    @pl.when(high != 0)
    def _():
        joined_ref[0:rows] = other_ref[...].astype(joined_ref.dtype)
        joined_ref[rows:] = mine_ref[...].astype(joined_ref.dtype)


def total_and_join(high, pieces, mine, other):
    return pl.pallas_call(
        total_and_join_kernel,
        out_shape=(
            jax.ShapeDtypeStruct((8, PIECE, CLEN), BF),
            jax.ShapeDtypeStruct((2 * mine.shape[0], CLEN), BF),
        ),
        in_specs=[pl.BlockSpec(memory_space=pltpu.SMEM), VM, VM, VM],
        out_specs=(VM, VM),
        compiler_params=SMALL,
        cost_estimate=pl.CostEstimate(flops=90000, bytes_accessed=500000, transcendentals=0),
    )(high, pieces, mine, other)


def finish_kernel(high_ref, pieces_ref, mine_ref, other_ref, prompt_ref, comp_ref, joined_ref):
    join(high_ref[0], mine_ref, other_ref, joined_ref)
    comp_ref[...] = joined_ref[0:DQK].astype(F32)
    for j in range(7):
        prompt_ref[PIECE * j : PIECE * (j + 1)] = pieces_ref[j].astype(F32)
    prompt_ref[PIECE * 7 : DQK] = pieces_ref[7, 0 : DQK - PIECE * 7].astype(F32)


def finish(high, pieces, mine, other):
    return pl.pallas_call(
        finish_kernel,
        out_shape=(jax.ShapeDtypeStruct((DQK, CLEN), F32), jax.ShapeDtypeStruct((DQK, CLEN), F32)),
        in_specs=[pl.BlockSpec(memory_space=pltpu.SMEM), VM, VM, VM],
        out_specs=(VM, VM),
        scratch_shapes=[pltpu.VMEM((WIDE, CLEN), BF)],
        compiler_params=SMALL,
        cost_estimate=pl.CostEstimate(flops=90000, bytes_accessed=900000, transcendentals=0),
    )(high, pieces, mine, other)


def swap(block, axis, count, bit):
    return lax.ppermute(block, axis, [(i, i ^ bit) for i in range(count)])


def on_device(queries, grad_out, prompt_kv, comp_kv, lengths):
    sample = lax.axis_index(CTX)
    live = lax.dynamic_slice(lengths, (sample,), (1,))
    prompt = lax.all_to_all(jnp.broadcast_to(prompt_kv[None], (8,) + prompt_kv.shape), HS, 0, 0)
    left = turn(queries, grad_out)
    terms, score_grad = main(live, queries, grad_out, left, prompt, comp_kv)
    terms = lax.all_to_all(terms, HS, 0, 0)
    grad_queries, token = query_grads(score_grad, prompt, comp_kv)
    prompt_part, comp = heads_sum(terms, token)
    x, yl = lax.axis_index("x"), lax.axis_index("yl")
    high = [(x & 1).reshape(1), (x >> 1).reshape(1), yl.reshape(1)]
    pieces = lax.all_to_all(prompt_part.reshape(8, PIECE, CLEN), "z", 0, 0)
    pieces, comp = total_and_join(high[0], pieces, comp, swap(comp, "x", 4, 1))
    pieces = lax.all_to_all(pieces, ("yh", "c"), 0, 0)
    pieces, comp = total_and_join(high[1], pieces, comp, swap(comp, "x", 4, 2))
    pieces = lax.all_to_all(pieces, "z", 0, 0)
    grad_prompt, grad_comp = finish(high[2], pieces, comp, swap(comp, "yl", 2, 1))
    return (grad_queries, grad_prompt, grad_comp)


def solution(mesh):
    parts = Mesh(mesh.devices.reshape(4, 8, 2, 2, 4), CTX + HS)
    in_specs = (P(CTX, HS), P(CTX, HS), P(None, HS), P(None, CTX), P())
    out_specs = (P(CTX, HS), P(None, HS), P(None, CTX))
    return jax.shard_map(
        on_device, mesh=parts, in_specs=in_specs, out_specs=out_specs, check_vma=False
    )
```

```python
import functools

import jax
import jax.numpy as jnp
from jax import lax
from jax.experimental import pallas as pl
from jax.experimental.pallas import tpu as pltpu
from jax.sharding import Mesh
from jax.sharding import PartitionSpec as P

D_LAT = 512
DQK = 576
CLEN = 128
HEADS = 8
KEYS = 1152
PROMPT = 1024
ROWS = CLEN * HEADS
WIDE = 640
PIECE = 80
EDGE = 64
HALF = 288
SLICE = 48
KEYS_AT = 1024
TALL = 9216
HS = ("yl", "x")
CTX = ("yh", "z", "c")
ORDER = (0, 2, 1, 3, 4, 6, 5, 7)

score_scale = 192.0 ** (-0.5)
LOG2E = 1.4426950408889634

BF = jnp.bfloat16
F32 = jnp.float32
VM = pl.BlockSpec(memory_space=pltpu.VMEM)
HBM = pl.BlockSpec(memory_space=pl.ANY)
PARAMS = pltpu.CompilerParams(vmem_limit_bytes=44 * 1024 * 1024)
SMALL = pltpu.CompilerParams(vmem_limit_bytes=4 * 1024 * 1024)


def dot(a, b, contract):
    return lax.dot_general(a, b, ((contract[0:1], contract[1:2]), ((), ())), preferred_element_type=F32)


def turn_kernel(q_ref, g_ref, left_ref):
    for i, h in enumerate(ORDER):
        part = q_ref[:, 1152 * (h // 2) + 512 * (h % 2) : 1152 * (h // 2) + 512 * (h % 2) + WIDE]
        turned = part.T
        first = 64 * (h % 2)
        left_ref[:, i * CLEN : (i + 1) * CLEN] = turned[first : first + DQK]
        left_ref[0:D_LAT, ROWS + i * CLEN : ROWS + (i + 1) * CLEN] = g_ref[:, D_LAT * h : D_LAT * (h + 1)].T
    left_ref[D_LAT:DQK, ROWS:] = jnp.zeros((DQK - D_LAT, ROWS), BF)


def turn(queries, grad_out):
    return pl.pallas_call(
        turn_kernel,
        out_shape=jax.ShapeDtypeStruct((DQK, 2 * ROWS), BF),
        in_specs=[VM, VM],
        out_specs=VM,
        compiler_params=PARAMS,
        cost_estimate=pl.CostEstimate(flops=0, bytes_accessed=4600000, transcendentals=0),
    )(queries, grad_out)


def after_kernel(block_ref, done_ref, out_ref):
    del block_ref, done_ref, out_ref


def after(block, done):
    return pl.pallas_call(
        after_kernel,
        out_shape=jax.ShapeDtypeStruct(block.shape, block.dtype),
        in_specs=[HBM, HBM],
        out_specs=HBM,
        input_output_aliases={0: 0},
        compiler_params=SMALL,
        cost_estimate=pl.CostEstimate(flops=0, bytes_accessed=0, transcendentals=0),
    )(block, done)


def main_kernel(lengths_ref, q_ref, g_ref, left_ref, mine_ref, other_ref, comp_ref, send_ref, keep_ref, tall_hbm, right_ref, keys_ref, score_ref, gprob_ref, sems):
    live, core = lengths_ref[lax.axis_index(CTX)], lax.axis_index("c")
    zero = jnp.zeros((EDGE, KEYS), BF)
    keys_ref[0:EDGE] = zero
    keys_ref[EDGE + DQK :] = zero
    for ref, half in ((mine_ref, core), (other_ref, 1 - core)):
        rows = pl.ds(pl.multiple_of(EDGE + HALF * half, 16), HALF)
        for j in range(8):
            keys_ref[rows, j * CLEN : (j + 1) * CLEN] = ref[j]
    keys_ref[EDGE : EDGE + DQK, PROMPT:] = comp_ref[...]
    pairs = [ORDER[2 * b : 2 * b + 2] for b in range(4)]

    def matmuls(b):
        odd = pairs[b][0] % 2
        starts = [1152 * (h // 2) + 512 * odd for h in pairs[b]]
        q = jnp.concatenate([q_ref[:, s : s + WIDE] for s in starts], axis=0)
        g = jnp.concatenate([g_ref[:, D_LAT * h : D_LAT * (h + 1)] for h in pairs[b]], axis=0)
        first = EDGE * (1 - odd)
        score_ref[256 * b : 256 * (b + 1)] = dot(q, keys_ref[first : first + WIDE], (1, 0))
        gprob_ref[256 * b : 256 * (b + 1)] = dot(g, keys_ref[EDGE : EDGE + D_LAT], (1, 0))

    def softmax(b):
        for r in range(256 * b, 256 * (b + 1), 16):
            slot = r % CLEN + lax.broadcasted_iota(jnp.int32, (16, CLEN), 0)
            own = lax.broadcasted_iota(jnp.int32, (16, CLEN), 1)
            score = score_ref[r : r + 16]
            tail = jnp.where(own <= slot, score[:, PROMPT:], -jnp.inf)
            score = jnp.concatenate([score[:, :PROMPT], tail], axis=1)
            largest = jnp.max(score, axis=1, keepdims=True)
            weight = jnp.exp2((score - largest) * (score_scale * LOG2E))
            total = jnp.sum(weight, axis=1, keepdims=True)
            alive = (slot[:, :1] < live).astype(F32)
            prob = weight * (alive / total)
            gprob = gprob_ref[r : r + 16]
            delta = jnp.sum(prob * gprob, axis=1, keepdims=True)
            right_ref[r : r + 16] = (prob * ((gprob - delta) * score_scale)).astype(BF)
            right_ref[ROWS + r : ROWS + r + 16] = prob.astype(BF)

    outs = []

    def send(source, target, sem):
        outs.append(pltpu.make_async_copy(source, target, sem))
        outs[-1].start()

    send(keys_ref, tall_hbm.at[pl.ds(KEYS_AT, DQK + 2 * EDGE)], sems.at[0])
    matmuls(0)
    matmuls(1)
    softmax(0)
    matmuls(2)
    softmax(1)
    matmuls(3)
    softmax(2)
    softmax(3)
    send(right_ref.at[pl.ds(0, ROWS)], tall_hbm.at[pl.ds(0, ROWS)], sems.at[1])
    for j in range(0, PROMPT, 256):
        part = dot(left_ref[...], right_ref[:, j : j + 256], (1, 0)).astype(BF)
        for k in range(2):
            top, low = part[:HALF, CLEN * k : CLEN * (k + 1)], part[HALF:, CLEN * k : CLEN * (k + 1)]
            send_ref[j // CLEN + k] = jnp.where(core == 0, low, top)
            keep_ref[j // CLEN + k, 0:HALF] = jnp.where(core == 0, top, low)
    part = dot(left_ref[...], right_ref[:, PROMPT:], (1, 0)).astype(BF)
    for k in range(8):
        rows = min(PIECE, DQK - PIECE * k)
        keep_ref[k, HALF : HALF + rows] = part[PIECE * k : PIECE * k + rows]
        if rows < PIECE:
            keep_ref[k, HALF + rows :] = jnp.zeros((PIECE - rows, CLEN), BF)
    for move in outs:
        move.wait()


def main(lengths, queries, grad_out, left, mine, other, comp):
    return pl.pallas_call(
        main_kernel,
        out_shape=(
            jax.ShapeDtypeStruct((8, HALF, CLEN), BF),
            jax.ShapeDtypeStruct((8, HALF + PIECE, CLEN), BF),
            jax.ShapeDtypeStruct((TALL, KEYS), BF),
        ),
        in_specs=[pl.BlockSpec(memory_space=pltpu.SMEM)] + [VM] * 6,
        out_specs=(VM, VM, HBM),
        scratch_shapes=[
            pltpu.VMEM((2 * ROWS, KEYS), BF),
            pltpu.VMEM((DQK + 2 * EDGE, KEYS), BF),
            pltpu.VMEM((ROWS, KEYS), F32),
            pltpu.VMEM((ROWS, KEYS), F32),
            pltpu.SemaphoreType.DMA((2,)),
        ],
        compiler_params=PARAMS,
        cost_estimate=pl.CostEstimate(flops=5200000000, bytes_accessed=12000000, transcendentals=1200000),
    )(lengths, queries, grad_out, left, mine, other, comp)


def query_kernel(tall_hbm, out_hbm, same_hbm, grad_ref, keys_ref, out_ref, in_sems, out_sems):
    del same_hbm
    loads = [pltpu.make_async_copy(tall_hbm.at[pl.ds(KEYS_AT, DQK + 2 * EDGE)], keys_ref, in_sems.at[2])]
    for b in range(2):
        rows = pl.ds(512 * b, 512)
        loads.append(pltpu.make_async_copy(tall_hbm.at[rows], grad_ref.at[rows], in_sems.at[b]))
    for load in loads:
        load.start()
    loads[0].wait()
    outs = []
    for b in range(2):
        loads[b + 1].wait()
        even = dot(grad_ref[512 * b : 512 * b + 256], keys_ref[EDGE:], (1, 1))
        odd = dot(grad_ref[512 * b + 256 : 512 * b + 512], keys_ref[:WIDE], (1, 1))
        for i in range(2):
            start = 1152 * (2 * b + i)
            e, o = even[128 * i : 128 * (i + 1)], odd[128 * i : 128 * (i + 1)]
            out_ref[:, start : start + 512] = e[:, :512].astype(BF)
            out_ref[:, start + 512 : start + 640] = (e[:, 512:] + o[:, :128]).astype(BF)
            out_ref[:, start + 640 : start + 1152] = o[:, 128:].astype(BF)
        columns = pl.ds(2304 * b, 2304)
        outs.append(pltpu.make_async_copy(out_ref.at[:, columns], out_hbm.at[:, columns], out_sems.at[b]))
        outs[-1].start()
    for move in outs:
        move.wait()


def query_grads(tall):
    return pl.pallas_call(
        query_kernel,
        out_shape=(jax.ShapeDtypeStruct((CLEN, HEADS * DQK), BF), jax.ShapeDtypeStruct(tall.shape, BF)),
        in_specs=[HBM],
        out_specs=(HBM, HBM),
        input_output_aliases={0: 1},
        scratch_shapes=[
            pltpu.VMEM((ROWS, KEYS), BF),
            pltpu.VMEM((DQK + 2 * EDGE, KEYS), BF),
            pltpu.VMEM((CLEN, HEADS * DQK), BF),
            pltpu.SemaphoreType.DMA((3,)),
            pltpu.SemaphoreType.DMA((2,)),
        ],
        compiler_params=PARAMS,
        cost_estimate=pl.CostEstimate(flops=1400000000, bytes_accessed=5000000, transcendentals=0),
    )(tall)


def cores_sum_kernel(keep_ref, got_ref, out_ref):
    for j in range(8):
        out_ref[j, 0:HALF] = (keep_ref[j, 0:HALF].astype(F32) + got_ref[j].astype(F32)).astype(BF)
        out_ref[j, HALF:] = keep_ref[j, HALF:]


def cores_sum(keep, got):
    return pl.pallas_call(
        cores_sum_kernel,
        out_shape=jax.ShapeDtypeStruct(keep.shape, BF),
        in_specs=[VM, VM],
        out_specs=VM,
        compiler_params=SMALL,
        cost_estimate=pl.CostEstimate(flops=300000, bytes_accessed=2100000, transcendentals=0),
    )(keep, got)


def total_of(ref, first, rows):
    total = ref[0, first : first + rows].astype(F32)
    for j in range(1, ref.shape[0]):
        total = total + ref[j, first : first + rows].astype(F32)
    return total


def heads_sum_kernel(terms_ref, tall_hbm, prompt_ref, comp_ref):
    del tall_hbm
    prompt_ref[0:HALF] = total_of(terms_ref, 0, HALF).astype(BF)
    prompt_ref[HALF:] = jnp.zeros((8 * SLICE - HALF, CLEN), BF)
    comp_ref[...] = total_of(terms_ref, HALF, PIECE).astype(BF)


def heads_sum(terms, tall):
    return pl.pallas_call(
        heads_sum_kernel,
        out_shape=(jax.ShapeDtypeStruct((8 * SLICE, CLEN), BF), jax.ShapeDtypeStruct((PIECE, CLEN), BF)),
        in_specs=[VM, HBM],
        out_specs=(VM, VM),
        compiler_params=PARAMS,
        cost_estimate=pl.CostEstimate(flops=400000, bytes_accessed=900000, transcendentals=0),
    )(terms, tall)


def join(bit, mine_ref, other_ref, joined_ref):
    axis, value = (("x", 1), ("x", 2), ("yl", 1))[bit]
    high = lax.axis_index(axis) & value
    rows = mine_ref.shape[0]
    mine, other = mine_ref[...].astype(joined_ref.dtype), other_ref[...].astype(joined_ref.dtype)
    joined_ref[0:rows] = jnp.where(high == 0, mine, other)
    joined_ref[rows:] = jnp.where(high == 0, other, mine)


def total_and_join_kernel(bit, pieces_ref, mine_ref, other_ref, out_ref, joined_ref):
    total = total_of(pieces_ref, 0, SLICE).astype(out_ref.dtype)
    for j in range(out_ref.shape[0]):
        out_ref[j] = total
    join(bit, mine_ref, other_ref, joined_ref)


def total_and_join(bit, pieces, mine, other, copies, kind):
    return pl.pallas_call(
        functools.partial(total_and_join_kernel, bit),
        out_shape=(
            jax.ShapeDtypeStruct((copies, SLICE, CLEN), kind),
            jax.ShapeDtypeStruct((2 * mine.shape[0], CLEN), BF),
        ),
        in_specs=[VM, VM, VM],
        out_specs=(VM, VM),
        compiler_params=SMALL,
        cost_estimate=pl.CostEstimate(flops=90000, bytes_accessed=500000, transcendentals=0),
    )(pieces, mine, other)


def finish_kernel(pieces_ref, mine_ref, other_ref, prompt_ref, comp_ref, joined_ref):
    join(2, mine_ref, other_ref, joined_ref)
    comp_ref[...] = joined_ref[0:DQK].astype(F32)
    for core in range(2):
        for j in range(HALF // SLICE):
            first = HALF * core + SLICE * j
            prompt_ref[first : first + SLICE] = pieces_ref[2 * j + core].astype(F32)


def finish(pieces, mine, other):
    return pl.pallas_call(
        finish_kernel,
        out_shape=(jax.ShapeDtypeStruct((DQK, CLEN), F32), jax.ShapeDtypeStruct((DQK, CLEN), F32)),
        in_specs=[VM, VM, VM],
        out_specs=(VM, VM),
        scratch_shapes=[pltpu.VMEM((WIDE, CLEN), BF)],
        compiler_params=SMALL,
        cost_estimate=pl.CostEstimate(flops=90000, bytes_accessed=900000, transcendentals=0),
    )(pieces, mine, other)


def swap(block, axis, count, bit):
    return lax.ppermute(block, axis, [(i, i ^ bit) for i in range(count)])


def on_device(queries, grad_out, prompt_kv, comp_kv, lengths):
    half = lax.dynamic_slice(prompt_kv, (HALF * lax.axis_index("c"), 0), (HALF, CLEN))
    mine = lax.all_to_all(jnp.broadcast_to(half[None], (8, HALF, CLEN)), HS, 0, 0)
    left = turn(queries, grad_out)
    mine = after(mine, left)
    other = swap(mine, "c", 2, 1)
    send, keep, tall = main(lengths, queries, grad_out, left, mine, other, comp_kv)
    terms = lax.all_to_all(cores_sum(keep, swap(send, "c", 2, 1)), HS, 0, 0)
    grad_queries, tall = query_grads(tall)
    prompt_part, comp = heads_sum(terms, tall)
    pieces = lax.all_to_all(prompt_part.reshape(8, SLICE, CLEN), "z", 0, 0)
    pieces, comp = total_and_join(0, pieces, comp, swap(comp, "x", 4, 1), 4, F32)
    pieces = lax.all_to_all(pieces, "yh", 0, 0)
    pieces, comp = total_and_join(1, pieces, comp, swap(comp, "x", 4, 2), 16, BF)
    pieces = lax.all_to_all(pieces, ("z", "c"), 0, 0)
    grad_prompt, grad_comp = finish(pieces, comp, swap(comp, "yl", 2, 1))
    return (grad_queries, grad_prompt, grad_comp)


def solution(mesh):
    parts = Mesh(mesh.devices.reshape(4, 8, 2, 2, 4), CTX + HS)
    in_specs = (P(CTX, HS), P(CTX, HS), P(None, HS), P(None, CTX), P())
    out_specs = (P(CTX, HS), P(None, HS), P(None, CTX))
    return jax.shard_map(
        on_device, mesh=parts, in_specs=in_specs, out_specs=out_specs, check_vma=False
    )
```

```python
import functools

import jax
import jax.numpy as jnp
from jax import lax
from jax.experimental import pallas as pl
from jax.experimental.pallas import tpu as pltpu
from jax.sharding import Mesh
from jax.sharding import PartitionSpec as P

D_LAT = 512
DQK = 576
CLEN = 128
HEADS = 8
KEYS = 1152
PROMPT = 1024
ROWS = CLEN * HEADS
WIDE = 640
PIECE = 80
EDGE = 64
HALF = 288
SLICE = 48
KEYS_AT = 1024
TALL = 9216
HS = ("yl", "x")
CTX = ("yh", "z", "c")
ORDER = (0, 2, 1, 3, 4, 6, 5, 7)

score_scale = 192.0 ** (-0.5)
LOG2E = 1.4426950408889634

BF = jnp.bfloat16
F32 = jnp.float32
VM = pl.BlockSpec(memory_space=pltpu.VMEM)
HBM = pl.BlockSpec(memory_space=pl.ANY)
PARAMS = pltpu.CompilerParams(vmem_limit_bytes=44 * 1024 * 1024)
SMALL = pltpu.CompilerParams(vmem_limit_bytes=4 * 1024 * 1024)


def dot(a, b, contract):
    return lax.dot_general(a, b, ((contract[0:1], contract[1:2]), ((), ())), preferred_element_type=F32)


def turn_kernel(lengths_ref, q_ref, g_ref, left_ref, alive_ref):
    slot = lax.broadcasted_iota(jnp.int32, (CLEN, CLEN), 0)
    alive_ref[...] = (slot < lengths_ref[lax.axis_index(CTX)]).astype(F32)
    for i, h in enumerate(ORDER):
        part = q_ref[:, 1152 * (h // 2) + 512 * (h % 2) : 1152 * (h // 2) + 512 * (h % 2) + WIDE]
        turned = part.T
        first = 64 * (h % 2)
        left_ref[:, i * CLEN : (i + 1) * CLEN] = turned[first : first + DQK]
        left_ref[0:D_LAT, ROWS + i * CLEN : ROWS + (i + 1) * CLEN] = g_ref[:, D_LAT * h : D_LAT * (h + 1)].T
    left_ref[D_LAT:DQK, ROWS:] = jnp.zeros((DQK - D_LAT, ROWS), BF)


def turn(lengths, queries, grad_out):
    return pl.pallas_call(
        turn_kernel,
        out_shape=(jax.ShapeDtypeStruct((DQK, 2 * ROWS), BF), jax.ShapeDtypeStruct((CLEN, CLEN), F32)),
        in_specs=[pl.BlockSpec(memory_space=pltpu.SMEM), VM, VM],
        out_specs=(VM, VM),
        compiler_params=PARAMS,
        cost_estimate=pl.CostEstimate(flops=0, bytes_accessed=4600000, transcendentals=0),
    )(lengths, queries, grad_out)


def after_kernel(block_ref, done_ref, out_ref):
    del block_ref, done_ref, out_ref


def after(block, done):
    return pl.pallas_call(
        after_kernel,
        out_shape=jax.ShapeDtypeStruct(block.shape, block.dtype),
        in_specs=[HBM, HBM],
        out_specs=HBM,
        input_output_aliases={0: 0},
        compiler_params=SMALL,
        cost_estimate=pl.CostEstimate(flops=0, bytes_accessed=0, transcendentals=0),
    )(block, done)


def main_kernel(alive_ref, q_ref, g_ref, left_ref, mine_ref, other_ref, comp_ref, send_ref, keep_ref, tall_hbm, right_ref, keys_ref, score_ref, gprob_ref, sems):
    core = lax.axis_index("c")
    zero = jnp.zeros((EDGE, KEYS), BF)
    keys_ref[0:EDGE] = zero
    keys_ref[EDGE + DQK :] = zero
    for ref, half in ((mine_ref, core), (other_ref, 1 - core)):
        rows = pl.ds(pl.multiple_of(EDGE + HALF * half, 16), HALF)
        for j in range(8):
            keys_ref[rows, j * CLEN : (j + 1) * CLEN] = ref[j]
    keys_ref[EDGE : EDGE + DQK, PROMPT:] = comp_ref[...]
    pairs = [ORDER[2 * b : 2 * b + 2] for b in range(4)]

    def matmuls(b):
        odd = pairs[b][0] % 2
        starts = [1152 * (h // 2) + 512 * odd for h in pairs[b]]
        q = jnp.concatenate([q_ref[:, s : s + WIDE] for s in starts], axis=0)
        g = jnp.concatenate([g_ref[:, D_LAT * h : D_LAT * (h + 1)] for h in pairs[b]], axis=0)
        first = EDGE * (1 - odd)
        score_ref[256 * b : 256 * (b + 1)] = dot(q, keys_ref[first : first + WIDE], (1, 0))
        gprob_ref[256 * b : 256 * (b + 1)] = dot(g, keys_ref[EDGE : EDGE + D_LAT], (1, 0))

    def softmax(b):
        for r in range(256 * b, 256 * (b + 1), 16):
            slot = r % CLEN + lax.broadcasted_iota(jnp.int32, (16, CLEN), 0)
            own = lax.broadcasted_iota(jnp.int32, (16, CLEN), 1)
            score = score_ref[r : r + 16]
            tail = jnp.where(own <= slot, score[:, PROMPT:], -jnp.inf)
            score = jnp.concatenate([score[:, :PROMPT], tail], axis=1)
            largest = jnp.max(score, axis=1, keepdims=True)
            weight = jnp.exp2((score - largest) * (score_scale * LOG2E))
            total = jnp.sum(weight, axis=1, keepdims=True)
            alive = alive_ref[r % CLEN : r % CLEN + 16, :1]
            prob = weight * (alive / total)
            gprob = gprob_ref[r : r + 16]
            delta = jnp.sum(prob * gprob, axis=1, keepdims=True)
            right_ref[r : r + 16] = (prob * ((gprob - delta) * score_scale)).astype(BF)
            right_ref[ROWS + r : ROWS + r + 16] = prob.astype(BF)

    outs = []

    def send(source, target, sem):
        outs.append(pltpu.make_async_copy(source, target, sem))
        outs[-1].start()

    send(keys_ref, tall_hbm.at[pl.ds(KEYS_AT, DQK + 2 * EDGE)], sems.at[0])
    matmuls(0)
    matmuls(1)
    softmax(0)
    matmuls(2)
    softmax(1)
    matmuls(3)
    softmax(2)
    softmax(3)
    send(right_ref.at[pl.ds(0, ROWS)], tall_hbm.at[pl.ds(0, ROWS)], sems.at[1])
    for j in range(0, PROMPT, 256):
        part = dot(left_ref[...], right_ref[:, j : j + 256], (1, 0)).astype(BF)
        for k in range(2):
            top, low = part[:HALF, CLEN * k : CLEN * (k + 1)], part[HALF:, CLEN * k : CLEN * (k + 1)]
            send_ref[j // CLEN + k] = jnp.where(core == 0, low, top)
            keep_ref[j // CLEN + k, 0:HALF] = jnp.where(core == 0, top, low)
    part = dot(left_ref[...], right_ref[:, PROMPT:], (1, 0)).astype(BF)
    for k in range(8):
        rows = min(PIECE, DQK - PIECE * k)
        keep_ref[k, HALF : HALF + rows] = part[PIECE * k : PIECE * k + rows]
        if rows < PIECE:
            keep_ref[k, HALF + rows :] = jnp.zeros((PIECE - rows, CLEN), BF)
    for move in outs:
        move.wait()


def main(alive, queries, grad_out, left, mine, other, comp):
    return pl.pallas_call(
        main_kernel,
        out_shape=(
            jax.ShapeDtypeStruct((8, HALF, CLEN), BF),
            jax.ShapeDtypeStruct((8, HALF + PIECE, CLEN), BF),
            jax.ShapeDtypeStruct((TALL, KEYS), BF),
        ),
        in_specs=[VM] * 7,
        out_specs=(VM, VM, HBM),
        scratch_shapes=[
            pltpu.VMEM((2 * ROWS, KEYS), BF),
            pltpu.VMEM((DQK + 2 * EDGE, KEYS), BF),
            pltpu.VMEM((ROWS, KEYS), F32),
            pltpu.VMEM((ROWS, KEYS), F32),
            pltpu.SemaphoreType.DMA((2,)),
        ],
        compiler_params=PARAMS,
        cost_estimate=pl.CostEstimate(flops=5200000000, bytes_accessed=12000000, transcendentals=1200000),
    )(alive, queries, grad_out, left, mine, other, comp)


def query_kernel(tall_hbm, out_hbm, same_hbm, grad_ref, keys_ref, out_ref, in_sems, out_sems):
    del same_hbm
    loads = [pltpu.make_async_copy(tall_hbm.at[pl.ds(KEYS_AT, DQK + 2 * EDGE)], keys_ref, in_sems.at[2])]
    for b in range(2):
        rows = pl.ds(512 * b, 512)
        loads.append(pltpu.make_async_copy(tall_hbm.at[rows], grad_ref.at[rows], in_sems.at[b]))
    for load in loads:
        load.start()
    loads[0].wait()
    outs = []
    for b in range(2):
        loads[b + 1].wait()
        even = dot(grad_ref[512 * b : 512 * b + 256], keys_ref[EDGE:], (1, 1))
        odd = dot(grad_ref[512 * b + 256 : 512 * b + 512], keys_ref[:WIDE], (1, 1))
        for i in range(2):
            start = 1152 * (2 * b + i)
            e, o = even[128 * i : 128 * (i + 1)], odd[128 * i : 128 * (i + 1)]
            out_ref[:, start : start + 512] = e[:, :512].astype(BF)
            out_ref[:, start + 512 : start + 640] = (e[:, 512:] + o[:, :128]).astype(BF)
            out_ref[:, start + 640 : start + 1152] = o[:, 128:].astype(BF)
        columns = pl.ds(2304 * b, 2304)
        outs.append(pltpu.make_async_copy(out_ref.at[:, columns], out_hbm.at[:, columns], out_sems.at[b]))
        outs[-1].start()
    for move in outs:
        move.wait()


def query_grads(tall):
    return pl.pallas_call(
        query_kernel,
        out_shape=(jax.ShapeDtypeStruct((CLEN, HEADS * DQK), BF), jax.ShapeDtypeStruct(tall.shape, BF)),
        in_specs=[HBM],
        out_specs=(HBM, HBM),
        input_output_aliases={0: 1},
        scratch_shapes=[
            pltpu.VMEM((ROWS, KEYS), BF),
            pltpu.VMEM((DQK + 2 * EDGE, KEYS), BF),
            pltpu.VMEM((CLEN, HEADS * DQK), BF),
            pltpu.SemaphoreType.DMA((3,)),
            pltpu.SemaphoreType.DMA((2,)),
        ],
        compiler_params=PARAMS,
        cost_estimate=pl.CostEstimate(flops=1400000000, bytes_accessed=5000000, transcendentals=0),
    )(tall)


def cores_sum_kernel(keep_ref, got_ref, out_ref):
    for j in range(8):
        out_ref[j, 0:HALF] = (keep_ref[j, 0:HALF].astype(F32) + got_ref[j].astype(F32)).astype(BF)
        out_ref[j, HALF:] = keep_ref[j, HALF:]


def cores_sum(keep, got):
    return pl.pallas_call(
        cores_sum_kernel,
        out_shape=jax.ShapeDtypeStruct(keep.shape, BF),
        in_specs=[VM, VM],
        out_specs=VM,
        compiler_params=SMALL,
        cost_estimate=pl.CostEstimate(flops=300000, bytes_accessed=2100000, transcendentals=0),
    )(keep, got)


def total_of(ref, first, rows):
    total = ref[0, first : first + rows].astype(F32)
    for j in range(1, ref.shape[0]):
        total = total + ref[j, first : first + rows].astype(F32)
    return total


def heads_sum_kernel(terms_ref, tall_hbm, prompt_ref, comp_ref):
    del tall_hbm
    prompt_ref[0:HALF] = total_of(terms_ref, 0, HALF).astype(BF)
    prompt_ref[HALF:] = jnp.zeros((8 * SLICE - HALF, CLEN), BF)
    comp_ref[0] = total_of(terms_ref, HALF, PIECE).astype(BF)


def heads_sum(terms, tall):
    return pl.pallas_call(
        heads_sum_kernel,
        out_shape=(jax.ShapeDtypeStruct((8 * SLICE, CLEN), BF), jax.ShapeDtypeStruct((1, PIECE, CLEN), BF)),
        in_specs=[VM, HBM],
        out_specs=(VM, VM),
        compiler_params=PARAMS,
        cost_estimate=pl.CostEstimate(flops=400000, bytes_accessed=900000, transcendentals=0),
    )(terms, tall)


def spread_kernel(pieces_ref, out_ref):
    total = total_of(pieces_ref, 0, SLICE).astype(out_ref.dtype)
    for j in range(out_ref.shape[0]):
        out_ref[j] = total


def join_kernel(axis, pieces_ref, mine_ref, other_ref, out_ref, joined_ref):
    spread_kernel(pieces_ref, out_ref)
    even = (lax.axis_index(axis) & 1) == 0
    count = mine_ref.shape[0]
    for k in range(count):
        mine, other = mine_ref[k].astype(F32), other_ref[k].astype(F32)
        joined_ref[k] = jnp.where(even, mine, other).astype(BF)
        joined_ref[count + k] = jnp.where(even, other, mine).astype(BF)


def sum_and_join(axis, pieces, copies, kind, mine, other):
    return pl.pallas_call(
        functools.partial(join_kernel, axis),
        out_shape=(
            jax.ShapeDtypeStruct((copies, SLICE, CLEN), kind),
            jax.ShapeDtypeStruct((2 * mine.shape[0], PIECE, CLEN), BF),
        ),
        in_specs=[VM, VM, VM],
        out_specs=(VM, VM),
        compiler_params=SMALL,
        cost_estimate=pl.CostEstimate(flops=90000, bytes_accessed=500000, transcendentals=0),
    )(pieces, mine, other)


def finish_kernel(pieces_ref, mine_ref, other_ref, prompt_ref, comp_ref):
    low = (lax.axis_index("x") & 2) == 0
    for odd in range(2):
        for yl in range(2):
            mine, other = mine_ref[2 * odd + yl].astype(F32), other_ref[2 * odd + yl].astype(F32)
            for high in range(2):
                first = PIECE * (4 * yl + 2 * high + odd)
                rows = min(PIECE, DQK - first)
                chunk = jnp.where(low, other, mine) if high else jnp.where(low, mine, other)
                comp_ref[first : first + rows] = chunk[:rows]
    for core in range(2):
        for j in range(HALF // SLICE):
            first = HALF * core + SLICE * j
            prompt_ref[first : first + SLICE] = pieces_ref[2 * j + core].astype(F32)


def finish(pieces, mine, other):
    return pl.pallas_call(
        finish_kernel,
        out_shape=(jax.ShapeDtypeStruct((DQK, CLEN), F32), jax.ShapeDtypeStruct((DQK, CLEN), F32)),
        in_specs=[VM, VM, VM],
        out_specs=(VM, VM),
        compiler_params=SMALL,
        cost_estimate=pl.CostEstimate(flops=90000, bytes_accessed=900000, transcendentals=0),
    )(pieces, mine, other)


def swap(block, axis, count, bit):
    return lax.ppermute(block, axis, [(i, i ^ bit) for i in range(count)])


def on_device(queries, grad_out, prompt_kv, comp_kv, lengths):
    half = lax.dynamic_slice(prompt_kv, (HALF * lax.axis_index("c"), 0), (HALF, CLEN))
    mine = lax.all_to_all(jnp.broadcast_to(half[None], (8, HALF, CLEN)), HS, 0, 0)
    left, alive = turn(lengths, queries, grad_out)
    mine = after(mine, left)
    other = swap(mine, "c", 2, 1)
    send, keep, tall = main(alive, queries, grad_out, left, mine, other, comp_kv)
    terms = lax.all_to_all(cores_sum(keep, swap(send, "c", 2, 1)), HS, 0, 0)
    grad_queries, tall = query_grads(tall)
    prompt_part, comp = heads_sum(terms, tall)
    pieces = lax.all_to_all(prompt_part.reshape(8, SLICE, CLEN), "z", 0, 0)
    pieces, comp = sum_and_join("yl", pieces, 4, F32, comp, swap(comp, "yl", 2, 1))
    pieces = lax.all_to_all(pieces, "yh", 0, 0)
    pieces, comp = sum_and_join("x", pieces, 16, BF, comp, swap(comp, "x", 4, 1))
    pieces = lax.all_to_all(pieces, ("z", "c"), 0, 0)
    grad_prompt, grad_comp = finish(pieces, comp, swap(comp, "x", 4, 2))
    return (grad_queries, grad_prompt, grad_comp)


def solution(mesh):
    parts = Mesh(mesh.devices.reshape(4, 8, 2, 2, 4), CTX + HS)
    in_specs = (P(CTX, HS), P(CTX, HS), P(None, HS), P(None, CTX), P())
    out_specs = (P(CTX, HS), P(None, HS), P(None, CTX))
    return jax.shard_map(
        on_device, mesh=parts, in_specs=in_specs, out_specs=out_specs, check_vma=False
    )
```

```python
import functools

import jax
import jax.numpy as jnp
from jax import lax
from jax.experimental import pallas as pl
from jax.experimental.pallas import tpu as pltpu
from jax.sharding import Mesh
from jax.sharding import PartitionSpec as P

D_LAT = 512
DQK = 576
CLEN = 128
HEADS = 8
KEYS = 1152
PROMPT = 1024
ROWS = CLEN * HEADS
WIDE = 640
PIECE = 80
EDGE = 64
HALF = 288
SLICE = 48
KEYS_AT = 1024
TALL = 9216
HS = ("yl", "x")
CTX = ("yh", "z", "c")
ORDER = (0, 2, 1, 3, 4, 6, 5, 7)

score_scale = 192.0 ** (-0.5)
LOG2E = 1.4426950408889634

BF = jnp.bfloat16
F32 = jnp.float32
VM = pl.BlockSpec(memory_space=pltpu.VMEM)
HBM = pl.BlockSpec(memory_space=pl.ANY)
PARAMS = pltpu.CompilerParams(vmem_limit_bytes=44 * 1024 * 1024)
SMALL = pltpu.CompilerParams(vmem_limit_bytes=4 * 1024 * 1024)


def dot(a, b, contract):
    return lax.dot_general(a, b, ((contract[0:1], contract[1:2]), ((), ())), preferred_element_type=F32)


def turn_kernel(lengths_ref, q_ref, g_ref, left_ref, alive_ref):
    slot = lax.broadcasted_iota(jnp.int32, (CLEN, CLEN), 0)
    alive_ref[...] = (slot < lengths_ref[lax.axis_index(CTX)]).astype(F32)
    for i, h in enumerate(ORDER):
        part = q_ref[:, 1152 * (h // 2) + 512 * (h % 2) : 1152 * (h // 2) + 512 * (h % 2) + WIDE]
        turned = part.T
        first = 64 * (h % 2)
        left_ref[:, i * CLEN : (i + 1) * CLEN] = turned[first : first + DQK]
        left_ref[0:D_LAT, ROWS + i * CLEN : ROWS + (i + 1) * CLEN] = g_ref[:, D_LAT * h : D_LAT * (h + 1)].T
    left_ref[D_LAT:DQK, ROWS:] = jnp.zeros((DQK - D_LAT, ROWS), BF)


def turn(lengths, queries, grad_out):
    return pl.pallas_call(
        turn_kernel,
        out_shape=(jax.ShapeDtypeStruct((DQK, 2 * ROWS), BF), jax.ShapeDtypeStruct((CLEN, CLEN), F32)),
        in_specs=[pl.BlockSpec(memory_space=pltpu.SMEM), VM, VM],
        out_specs=(VM, VM),
        compiler_params=PARAMS,
        cost_estimate=pl.CostEstimate(flops=0, bytes_accessed=4600000, transcendentals=0),
    )(lengths, queries, grad_out)


def after_kernel(block_ref, done_ref, out_ref):
    del block_ref, done_ref, out_ref


def after(block, done):
    return pl.pallas_call(
        after_kernel,
        out_shape=jax.ShapeDtypeStruct(block.shape, block.dtype),
        in_specs=[HBM, HBM],
        out_specs=HBM,
        input_output_aliases={0: 0},
        compiler_params=SMALL,
        cost_estimate=pl.CostEstimate(flops=0, bytes_accessed=0, transcendentals=0),
    )(block, done)


def main_kernel(alive_ref, q_ref, g_ref, left_ref, mine_ref, other_ref, comp_ref, send_ref, keep_ref, tall_hbm, right_ref, keys_ref, score_ref, gprob_ref, sems):
    core = lax.axis_index("c")
    zero = jnp.zeros((EDGE, KEYS), BF)
    keys_ref[0:EDGE] = zero
    keys_ref[EDGE + DQK :] = zero
    for ref, half in ((mine_ref, core), (other_ref, 1 - core)):
        rows = pl.ds(pl.multiple_of(EDGE + HALF * half, 16), HALF)
        for j in range(8):
            keys_ref[rows, j * CLEN : (j + 1) * CLEN] = ref[j]
    keys_ref[EDGE : EDGE + DQK, PROMPT:] = comp_ref[...]
    pairs = [ORDER[2 * b : 2 * b + 2] for b in range(4)]

    def matmuls(b):
        odd = pairs[b][0] % 2
        starts = [1152 * (h // 2) + 512 * odd for h in pairs[b]]
        q = jnp.concatenate([q_ref[:, s : s + WIDE] for s in starts], axis=0)
        g = jnp.concatenate([g_ref[:, D_LAT * h : D_LAT * (h + 1)] for h in pairs[b]], axis=0)
        first = EDGE * (1 - odd)
        score_ref[256 * b : 256 * (b + 1)] = dot(q, keys_ref[first : first + WIDE], (1, 0))
        gprob_ref[256 * b : 256 * (b + 1)] = dot(g, keys_ref[EDGE : EDGE + D_LAT], (1, 0))

    def softmax(b):
        for r in range(256 * b, 256 * (b + 1), 16):
            slot = r % CLEN + lax.broadcasted_iota(jnp.int32, (16, CLEN), 0)
            own = lax.broadcasted_iota(jnp.int32, (16, CLEN), 1)
            score = score_ref[r : r + 16]
            tail = jnp.where(own <= slot, score[:, PROMPT:], -jnp.inf)
            score = jnp.concatenate([score[:, :PROMPT], tail], axis=1)
            largest = jnp.max(score, axis=1, keepdims=True)
            weight = jnp.exp2((score - largest) * (score_scale * LOG2E))
            total = jnp.sum(weight, axis=1, keepdims=True)
            alive = alive_ref[r % CLEN : r % CLEN + 16, :1]
            prob = weight * (alive / total)
            gprob = gprob_ref[r : r + 16]
            delta = jnp.sum(prob * gprob, axis=1, keepdims=True)
            right_ref[r : r + 16] = (prob * ((gprob - delta) * score_scale)).astype(BF)
            right_ref[ROWS + r : ROWS + r + 16] = prob.astype(BF)

    outs = []

    def send(source, target, sem):
        outs.append(pltpu.make_async_copy(source, target, sem))
        outs[-1].start()

    send(keys_ref, tall_hbm.at[pl.ds(KEYS_AT, DQK + 2 * EDGE)], sems.at[0])
    matmuls(0)
    matmuls(1)
    softmax(0)
    matmuls(2)
    softmax(1)
    matmuls(3)
    softmax(2)
    softmax(3)
    send(right_ref.at[pl.ds(0, ROWS)], tall_hbm.at[pl.ds(0, ROWS)], sems.at[1])
    for j in range(0, PROMPT, 256):
        part = dot(left_ref[...], right_ref[:, j : j + 256], (1, 0)).astype(BF)
        for k in range(2):
            top, low = part[:HALF, CLEN * k : CLEN * (k + 1)], part[HALF:, CLEN * k : CLEN * (k + 1)]
            send_ref[j // CLEN + k] = jnp.where(core == 0, low, top)
            keep_ref[j // CLEN + k, 0:HALF] = jnp.where(core == 0, top, low)
    part = dot(left_ref[...], right_ref[:, PROMPT:], (1, 0)).astype(BF)
    for k in range(8):
        rows = min(PIECE, DQK - PIECE * k)
        keep_ref[k, HALF : HALF + rows] = part[PIECE * k : PIECE * k + rows]
        if rows < PIECE:
            keep_ref[k, HALF + rows :] = jnp.zeros((PIECE - rows, CLEN), BF)
    for move in outs:
        move.wait()


def main(alive, queries, grad_out, left, mine, other, comp):
    return pl.pallas_call(
        main_kernel,
        out_shape=(
            jax.ShapeDtypeStruct((8, HALF, CLEN), BF),
            jax.ShapeDtypeStruct((8, HALF + PIECE, CLEN), BF),
            jax.ShapeDtypeStruct((TALL, KEYS), BF),
        ),
        in_specs=[VM] * 7,
        out_specs=(VM, VM, HBM),
        scratch_shapes=[
            pltpu.VMEM((2 * ROWS, KEYS), BF),
            pltpu.VMEM((DQK + 2 * EDGE, KEYS), BF),
            pltpu.VMEM((ROWS, KEYS), F32),
            pltpu.VMEM((ROWS, KEYS), F32),
            pltpu.SemaphoreType.DMA((2,)),
        ],
        compiler_params=PARAMS,
        cost_estimate=pl.CostEstimate(flops=5200000000, bytes_accessed=12000000, transcendentals=1200000),
    )(alive, queries, grad_out, left, mine, other, comp)


def query_kernel(tall_hbm, out_hbm, same_hbm, grad_ref, keys_ref, out_ref, in_sems, out_sems):
    del same_hbm
    loads = [pltpu.make_async_copy(tall_hbm.at[pl.ds(KEYS_AT, DQK + 2 * EDGE)], keys_ref, in_sems.at[2])]
    for b in range(2):
        rows = pl.ds(512 * b, 512)
        loads.append(pltpu.make_async_copy(tall_hbm.at[rows], grad_ref.at[rows], in_sems.at[b]))
    for load in loads:
        load.start()
    loads[0].wait()
    outs = []
    for b in range(2):
        loads[b + 1].wait()
        even = dot(grad_ref[512 * b : 512 * b + 256], keys_ref[EDGE:], (1, 1))
        odd = dot(grad_ref[512 * b + 256 : 512 * b + 512], keys_ref[:WIDE], (1, 1))
        for i in range(2):
            start = 1152 * (2 * b + i)
            e, o = even[128 * i : 128 * (i + 1)], odd[128 * i : 128 * (i + 1)]
            out_ref[:, start : start + 512] = e[:, :512].astype(BF)
            out_ref[:, start + 512 : start + 640] = (e[:, 512:] + o[:, :128]).astype(BF)
            out_ref[:, start + 640 : start + 1152] = o[:, 128:].astype(BF)
        columns = pl.ds(2304 * b, 2304)
        outs.append(pltpu.make_async_copy(out_ref.at[:, columns], out_hbm.at[:, columns], out_sems.at[b]))
        outs[-1].start()
    for move in outs:
        move.wait()


def query_grads(tall):
    return pl.pallas_call(
        query_kernel,
        out_shape=(jax.ShapeDtypeStruct((CLEN, HEADS * DQK), BF), jax.ShapeDtypeStruct(tall.shape, BF)),
        in_specs=[HBM],
        out_specs=(HBM, HBM),
        input_output_aliases={0: 1},
        scratch_shapes=[
            pltpu.VMEM((ROWS, KEYS), BF),
            pltpu.VMEM((DQK + 2 * EDGE, KEYS), BF),
            pltpu.VMEM((CLEN, HEADS * DQK), BF),
            pltpu.SemaphoreType.DMA((3,)),
            pltpu.SemaphoreType.DMA((2,)),
        ],
        compiler_params=PARAMS,
        cost_estimate=pl.CostEstimate(flops=1400000000, bytes_accessed=5000000, transcendentals=0),
    )(tall)


def cores_sum_kernel(keep_ref, got_ref, out_ref):
    for j in range(8):
        out_ref[j, 0:HALF] = (keep_ref[j, 0:HALF].astype(F32) + got_ref[j].astype(F32)).astype(BF)
        out_ref[j, HALF:] = keep_ref[j, HALF:]


def cores_sum(keep, got):
    return pl.pallas_call(
        cores_sum_kernel,
        out_shape=jax.ShapeDtypeStruct(keep.shape, BF),
        in_specs=[VM, VM],
        out_specs=VM,
        compiler_params=SMALL,
        cost_estimate=pl.CostEstimate(flops=300000, bytes_accessed=2100000, transcendentals=0),
    )(keep, got)


def total_of(ref, first, rows):
    total = ref[0, first : first + rows].astype(F32)
    for j in range(1, ref.shape[0]):
        total = total + ref[j, first : first + rows].astype(F32)
    return total


def heads_sum_kernel(terms_ref, tall_hbm, prompt_ref, comp_ref):
    del tall_hbm
    prompt_ref[0:HALF] = total_of(terms_ref, 0, HALF).astype(BF)
    prompt_ref[HALF:] = jnp.zeros((8 * SLICE - HALF, CLEN), BF)
    comp_ref[0] = total_of(terms_ref, HALF, PIECE).astype(BF)


def heads_sum(terms, tall):
    return pl.pallas_call(
        heads_sum_kernel,
        out_shape=(jax.ShapeDtypeStruct((8 * SLICE, CLEN), BF), jax.ShapeDtypeStruct((1, PIECE, CLEN), BF)),
        in_specs=[VM, HBM],
        out_specs=(VM, VM),
        compiler_params=PARAMS,
        cost_estimate=pl.CostEstimate(flops=400000, bytes_accessed=900000, transcendentals=0),
    )(terms, tall)


def spread_kernel(pieces_ref, out_ref):
    total = total_of(pieces_ref, 0, SLICE).astype(out_ref.dtype)
    for j in range(out_ref.shape[0]):
        out_ref[j] = total


def join_kernel(axis, pieces_ref, mine_ref, other_ref, out_ref, joined_ref):
    spread_kernel(pieces_ref, out_ref)
    even = (lax.axis_index(axis) & 1) == 0
    count = mine_ref.shape[0]
    for k in range(count):
        mine, other = mine_ref[k].astype(F32), other_ref[k].astype(F32)
        joined_ref[k] = jnp.where(even, mine, other).astype(BF)
        joined_ref[count + k] = jnp.where(even, other, mine).astype(BF)


def sum_and_join(axis, pieces, copies, kind, mine, other):
    return pl.pallas_call(
        functools.partial(join_kernel, axis),
        out_shape=(
            jax.ShapeDtypeStruct((copies, SLICE, CLEN), kind),
            jax.ShapeDtypeStruct((2 * mine.shape[0], PIECE, CLEN), BF),
        ),
        in_specs=[VM, VM, VM],
        out_specs=(VM, VM),
        compiler_params=SMALL,
        cost_estimate=pl.CostEstimate(flops=90000, bytes_accessed=500000, transcendentals=0),
    )(pieces, mine, other)


def finish_kernel(pieces_ref, mine_ref, other_ref, prompt_ref, comp_ref):
    low = (lax.axis_index("x") & 2) == 0
    for odd in range(2):
        for yl in range(2):
            mine, other = mine_ref[2 * odd + yl].astype(F32), other_ref[2 * odd + yl].astype(F32)
            for high in range(2):
                first = PIECE * (4 * yl + 2 * high + odd)
                rows = min(PIECE, DQK - first)
                chunk = jnp.where(low, other, mine) if high else jnp.where(low, mine, other)
                comp_ref[first : first + rows] = chunk[:rows]
    for core in range(2):
        for j in range(HALF // SLICE):
            first = HALF * core + SLICE * j
            prompt_ref[first : first + SLICE] = pieces_ref[8 * core + j].astype(F32)


def finish(pieces, mine, other):
    return pl.pallas_call(
        finish_kernel,
        out_shape=(jax.ShapeDtypeStruct((DQK, CLEN), F32), jax.ShapeDtypeStruct((DQK, CLEN), F32)),
        in_specs=[VM, VM, VM],
        out_specs=(VM, VM),
        compiler_params=SMALL,
        cost_estimate=pl.CostEstimate(flops=90000, bytes_accessed=900000, transcendentals=0),
    )(pieces, mine, other)


def swap(block, axis, count, bit):
    return lax.ppermute(block, axis, [(i, i ^ bit) for i in range(count)])


def on_device(queries, grad_out, prompt_kv, comp_kv, lengths):
    half = lax.dynamic_slice(prompt_kv, (HALF * lax.axis_index("c"), 0), (HALF, CLEN))
    mine = lax.all_to_all(jnp.broadcast_to(half[None], (8, HALF, CLEN)), HS, 0, 0)
    left, alive = turn(lengths, queries, grad_out)
    mine = after(mine, left)
    other = swap(mine, "c", 2, 1)
    send, keep, tall = main(alive, queries, grad_out, left, mine, other, comp_kv)
    terms = lax.all_to_all(cores_sum(keep, swap(send, "c", 2, 1)), HS, 0, 0)
    grad_queries, tall = query_grads(tall)
    prompt_part, comp = heads_sum(terms, tall)
    pieces = lax.all_to_all(prompt_part.reshape(8, SLICE, CLEN), "z", 0, 0)
    pieces, comp = sum_and_join("yl", pieces, 4, F32, comp, swap(comp, "yl", 2, 1))
    pieces = lax.all_to_all(pieces, "yh", 0, 0)
    pieces, comp = sum_and_join("x", pieces, 16, BF, comp, swap(comp, "x", 4, 1))
    pieces = lax.all_to_all(pieces, ("c", "z"), 0, 0)
    grad_prompt, grad_comp = finish(pieces, comp, swap(comp, "x", 4, 2))
    return (grad_queries, grad_prompt, grad_comp)


def solution(mesh):
    parts = Mesh(mesh.devices.reshape(4, 8, 2, 2, 4), CTX + HS)
    in_specs = (P(CTX, HS), P(CTX, HS), P(None, HS), P(None, CTX), P())
    out_specs = (P(CTX, HS), P(None, HS), P(None, CTX))
    return jax.shard_map(
        on_device, mesh=parts, in_specs=in_specs, out_specs=out_specs, check_vma=False
    )
```
